256 devices in a mesh: row: 16 (over x_hi, y, core), col: 16 (over x_lo, z).
Axes of the slice: x: 4 (x_hi: 2, x_lo: 2; x = x_hi * 2 + x_lo), y: 4, z: 8, core: 2. Of those that a mesh axis runs over, the one named last changes fastest.
Arguments:
- pair: bfloat16 [512, 512, 128], P('row', 'col'), may hold values from -6 to 6
- residue_mask: int32 [512], replicated, may hold values 0 or 1
- chain_index: int32 [512], replicated, may hold values from 0 to 3, as said below
- norm_gain: float32 [128], replicated, may hold values from 0.1 to 1.9
- norm_shift: float32 [128], replicated, may hold values from -3 to 3
- w_proj: bfloat16 [128, 512], replicated, may hold values from -1 to 1
- gate_shift: float32 [128], replicated, may hold values from -4 to 4
- w_bias: bfloat16 [128, 4], replicated, may hold values from -0.5 to 0.5
- inter_chain: float32 [4], replicated, may hold values from -2 to 2
- w_out: bfloat16 [128, 128], replicated, may hold values from -0.5 to 0.5
- out_shift: float32 [128], replicated, may hold values from -3 to 3
Outputs:
- update: bfloat16 [512, 512, 128], P('row', 'col')
The draws below stay inside these ranges and needn't reach their ends.
Inputs may be any that keep to these rules, and one draw needn't show every extreme that they name: `chain_index`: never falls along the residues; the first residue has chain 0 and the last chain 3.
All inputs are finite; a program needn't handle non-finite values.
Results may differ from the reference program's by a relative error of at most 0.0081.
Values may be sent and summed in bfloat16 or wider, within the bound.
No kernel may reach another device: no remote copies, remote signals or barrier semaphores. Data moves between devices by JAX's collectives and lax.ppermute only.
A program may use at most 128 MiB of HBM per device.

```python
import jax
import jax.numpy as jnp
from jax import lax

C = 128
H = 4
HD = 32
N = 512


def draw_chain_index(key, part):
    key = jax.random.fold_in(key, 11)
    breaks = jax.random.randint(key, (3,), 1, N)
    position = jnp.arange(N, dtype=jnp.int32)
    return jnp.sum((position[:, None] >= breaks[None, :]).astype(jnp.int32), axis=1).astype(jnp.int32)


def draw_pair(key, part):
    key = jax.random.fold_in(key, 23)
    key_noise = jax.random.fold_in(key, 0)
    values = jnp.clip(jax.random.normal(key_noise, (N, N, C), jnp.float32), -6.0, 6.0)
    return values.astype(jnp.bfloat16)


def draw_w_proj(key, part):
    key = jax.random.fold_in(key, 29)
    key_base = jax.random.fold_in(key, 0)
    width = H * HD
    values = jax.random.normal(key_base, (C, 4 * width), jnp.float32) * C ** (-0.5)
    return jnp.clip(values, -1.0, 1.0).astype(jnp.bfloat16)


def with_ends(values, rng, least, largest):
    shape = values.shape
    spot = [jax.random.randint(jax.random.fold_in(rng, axis), (), 0, shape[axis]) for axis in range(len(shape))]
    values = values.at[tuple(spot)].set(least)
    longest = shape.index(max(shape))
    spot[longest] = (spot[longest] + 1) % shape[longest]
    return values.at[tuple(spot)].set(largest)


def centred(stream_key, dims, deviation, limit, kind=jnp.bfloat16):
    values = jax.random.normal(stream_key, dims, jnp.float32) * deviation
    return jnp.minimum(jnp.maximum(values, -limit), limit).astype(kind)


def setup_inputs(seed: int = 0) -> dict:
    key_of = jax.random.split(jax.random.key(seed), 12)
    pair = draw_pair(jax.random.fold_in(key_of[11], 71), 0)
    residue_mask = with_ends((jax.random.randint(key_of[1], (N,), 0, 8) < 7).astype(jnp.int32), jax.random.fold_in(key_of[1], 1), 0, 1)
    chain_index = draw_chain_index(jax.random.fold_in(key_of[11], 71), 0)
    norm_gain = jnp.clip(1.0 + 0.18 * jax.random.normal(key_of[3], (C,), jnp.float32), 0.1, 1.9)
    norm_shift = centred(key_of[4], (C,), 0.5, 3.0, jnp.float32)
    w_proj = draw_w_proj(jax.random.fold_in(key_of[11], 71), 0)
    gate_shift = centred(key_of[6], (H * HD,), 1.0, 4.0, jnp.float32)
    w_bias = centred(key_of[7], (C, H), C ** -0.5, 0.5)
    inter_chain = jnp.clip(jax.random.uniform(key_of[8], (H,), jnp.float32, -2.0, 2.0), -2.0, 2.0)
    w_out = centred(key_of[9], (H * HD, C), (H * HD) ** -0.5, 0.5)
    out_shift = centred(key_of[10], (C,), 0.5, 3.0, jnp.float32)
    return {"pair": pair, "residue_mask": residue_mask, "chain_index": chain_index, "norm_gain": norm_gain, "norm_shift": norm_shift, "w_proj": w_proj, "gate_shift": gate_shift, "w_bias": w_bias, "inter_chain": inter_chain, "w_out": w_out, "out_shift": out_shift}


def layer_norm(pair, norm_gain, norm_shift):
    values = pair.astype(jnp.float32)
    center = lax.optimization_barrier(jnp.mean(values, axis=-1, keepdims=True))
    spread = lax.optimization_barrier(jnp.mean((values - center) ** 2, axis=-1, keepdims=True))
    return ((values - center) * lax.rsqrt(spread + 1e-05) * norm_gain + norm_shift).astype(jnp.bfloat16)

def reference(pair, residue_mask, chain_index, norm_gain, norm_shift, w_proj, gate_shift, w_bias, inter_chain, w_out, out_shift):
    width = H * HD
    normed = layer_norm(pair, norm_gain, norm_shift)
    flat = normed.reshape(N * N, C)
    proj = jnp.dot(flat, w_proj, preferred_element_type=jnp.float32)
    query = (proj[:, :width] / jnp.sqrt(jnp.float32(HD))).astype(jnp.bfloat16).reshape(N, N, H, HD)
    key_all = proj[:, width:2 * width].astype(jnp.bfloat16).reshape(N, N, H, HD)
    value_all = proj[:, 2 * width:3 * width].astype(jnp.bfloat16).reshape(N, N, H, HD)
    gate = jax.nn.sigmoid(proj[:, 3 * width:] + gate_shift)
    bias = jnp.einsum('abc,ch->hab', normed.astype(jnp.float32), w_bias.astype(jnp.float32)).astype(jnp.bfloat16)
    bias_ik = jnp.transpose(bias, (0, 2, 1)).astype(jnp.float32)
    cross = (chain_index[:, None] != chain_index[None, :]).astype(jnp.float32)
    extra = bias_ik + inter_chain[:, None, None] * cross[None]
    live = residue_mask > 0
    block = 8

    def one_block(index):
        start = (index * block).astype(jnp.int32)
        q_blk = lax.dynamic_slice_in_dim(query, start, block, 1).astype(jnp.float32)
        k_blk = lax.dynamic_slice_in_dim(key_all, start, block, 1).astype(jnp.float32)
        v_blk = lax.dynamic_slice_in_dim(value_all, start, block, 1).astype(jnp.float32)
        logits = jnp.einsum('ijhd,kjhd->jhik', q_blk, k_blk) + extra[None]
        logits = jnp.where(live[None, None, None, :], logits, jnp.float32(-1000000000.0))
        top = lax.optimization_barrier(jnp.max(logits, axis=-1, keepdims=True))
        expo = jnp.exp(logits - top)
        weights = expo / lax.optimization_barrier(jnp.sum(expo, axis=-1, keepdims=True))
        return jnp.einsum('jhik,kjhd->ijhd', weights, v_blk)
    blocks = lax.map(one_block, jnp.arange(N // block, dtype=jnp.int32))
    attended = jnp.transpose(blocks, (1, 0, 2, 3, 4)).reshape(N * N, width)
    gated = (gate * attended).astype(jnp.bfloat16)
    update = jnp.dot(gated, w_out, preferred_element_type=jnp.float32) + out_shift
    return update.astype(jnp.bfloat16).reshape(N, N, C)
```

```python
import functools
import math

import jax
import jax.numpy as jnp
from jax import lax
from jax.experimental import pallas as pl
from jax.experimental.pallas import tpu as pltpu
from jax.sharding import PartitionSpec as P

F32, BF16 = jnp.float32, jnp.bfloat16
NT = (((1,), (1,)), ((), ()))
DEAD = -1e30


def norm_kernel(core_ref, pair_ref, gain_ref, shift_ref, w_bias_ref, keep_ref, send_ref, bias_ref):
    rows, cols, channels = pair_ref.shape
    heads = w_bias_ref.shape[1]
    copies = bias_ref.shape[0]
    values = pair_ref[...].astype(F32)
    center = jnp.mean(values, axis=-1, keepdims=True)
    away = values - center
    spread = jnp.mean(away * away, axis=-1, keepdims=True)
    normed = away * lax.rsqrt(spread + 1e-05) * gain_ref[...] + shift_ref[...]
    flat = normed.reshape(rows * cols, channels).astype(BF16)
    lanes = heads * cols
    spot = (lax.broadcasted_iota(jnp.int32, (heads, lanes), 1) // cols) == lax.broadcasted_iota(
        jnp.int32, (heads, lanes), 0
    )
    wide = jnp.dot(w_bias_ref[...], spot.astype(BF16), preferred_element_type=F32).astype(BF16)
    every = jnp.dot(flat, wide, preferred_element_type=F32).reshape(rows, cols, lanes)
    own = (lax.broadcasted_iota(jnp.int32, (1, cols, lanes), 2) % cols) == lax.broadcasted_iota(
        jnp.int32, (1, cols, lanes), 1
    )
    bias = jnp.sum(jnp.where(own, every, 0.0), axis=1).astype(BF16)
    bias_ref[...] = jnp.broadcast_to(bias[None], (copies, rows, lanes))
    half = cols // 2
    turned = jnp.swapaxes(normed, 0, 1)
    first = core_ref[0] == 0
    keep_ref[...] = jnp.where(first, turned[:half], turned[half:]).astype(BF16)
    send_ref[...] = jnp.where(first, turned[half:], turned[:half]).astype(BF16)


def attend_kernel(
    place_ref,
    inter_ref,
    near_ref,
    far_ref,
    bias_ref,
    dead_ref,
    chain_ref,
    chain_query_ref,
    wk_ref,
    wv_ref,
    wqg_ref,
    gate_shift_ref,
    w_out_ref,
    out_shift_ref,
    keep_ref,
    send_ref,
    x_ref,
    extra_ref,
    gated_ref,
    *,
    heads,
):
    blocks, cols, rows, channels = near_ref.shape
    width = w_out_ref.shape[0]
    size = width // heads
    keys = x_ref.shape[1]
    lanes = heads * rows
    me = place_ref[0]
    first_query = pl.multiple_of((me // 2) * (2 * rows), 2 * rows)
    for step in range(2 * blocks):
        piece = near_ref if step < blocks else far_ref
        source = jnp.bitwise_xor(me, step)
        x_ref[:, pl.ds(pl.multiple_of(source * rows, rows), rows), :] = piece[step % blocks]

    lane = lax.broadcasted_iota(jnp.int32, (1, lanes), 1) // rows
    offset = jnp.zeros((1, lanes), F32)
    for head in range(heads):
        offset = jnp.where(lane == head, inter_ref[head], offset)
    for core in range(2):
        here = bias_ref[:, core].reshape(keys, lanes).astype(F32)
        cross = chain_ref[...] != chain_query_ref[:, core * lanes : (core + 1) * lanes]
        extra_ref[:, core * lanes : (core + 1) * lanes] = (
            here + jnp.where(cross, offset, 0.0)
        ) + dead_ref[...]

    query_head = lax.broadcasted_iota(jnp.int32, (1, channels), 1) // size
    head_rows = lax.broadcasted_iota(jnp.int32, (width, 2 * lanes), 0) // size
    head_lanes = (lax.broadcasted_iota(jnp.int32, (width, 2 * lanes), 1) % lanes) // rows
    own_head = head_rows == head_lanes
    fold_row = lax.broadcasted_iota(jnp.int32, (2 * rows, 2 * lanes), 0)
    fold_lane = lax.broadcasted_iota(jnp.int32, (2 * rows, 2 * lanes), 1)
    fold = (
        (fold_row // rows == fold_lane // lanes) & (fold_row % rows == fold_lane % rows)
    ).astype(F32).astype(BF16)
    ones = jnp.ones((16, keys), BF16)
    scale = 1.0 / math.sqrt(size)

    def column(j, carry):
        x = x_ref[j]
        key = jnp.dot(x, wk_ref[...], preferred_element_type=F32).astype(BF16)
        value = lax.dot_general(wv_ref[...], x, NT, preferred_element_type=F32).astype(BF16)
        mine = x_ref[j, pl.ds(first_query, 2 * rows), :]
        qg = jnp.dot(mine, wqg_ref[...], preferred_element_type=F32)
        query = qg[:, :width] * scale
        gate = jax.nn.sigmoid(qg[:, width:] + gate_shift_ref[...])
        spread = jnp.concatenate(
            [
                jnp.where(query_head == head, query[core * rows : (core + 1) * rows], 0.0)
                for core in range(2)
                for head in range(heads)
            ],
            axis=0,
        ).astype(BF16)
        logits = lax.dot_general(key, spread, NT, preferred_element_type=F32) + extra_ref[...]
        top = jnp.max(logits, axis=0, keepdims=True)
        expo = jnp.exp(logits - top).astype(BF16)
        both = jnp.dot(
            jnp.concatenate([value, ones], axis=0), expo, preferred_element_type=F32
        )
        part = jnp.where(own_head, both[:width], 0.0) / both[width : width + 1]
        high = part.astype(BF16)
        low = (part - high.astype(F32)).astype(BF16)
        attended = lax.dot_general(fold, high, NT, preferred_element_type=F32)
        attended += lax.dot_general(fold, low, NT, preferred_element_type=F32)
        gated_ref[j] = (gate * attended).astype(BF16)
        return carry

    lax.fori_loop(0, cols, column, 0, unroll=2)
    update = jnp.dot(
        gated_ref[...].reshape(cols * 2 * rows, width),
        w_out_ref[...],
        preferred_element_type=F32,
    )
    update = (update + out_shift_ref[...]).reshape(cols, 2 * rows, channels)
    turned = jnp.swapaxes(update, 0, 1)
    first = me % 2 == 0
    keep_ref[...] = jnp.where(first, turned[:rows], turned[rows:]).astype(BF16)
    send_ref[...] = jnp.where(first, turned[rows:], turned[:rows]).astype(BF16)


def whole():
    return pl.BlockSpec(memory_space=pltpu.VMEM)


def scalars():
    return pl.BlockSpec(memory_space=pltpu.SMEM)


def on_device(
    row_count,
    col_count,
    pair,
    residue_mask,
    chain_index,
    norm_gain,
    norm_shift,
    w_proj,
    gate_shift,
    w_bias,
    inter_chain,
    w_out,
    out_shift,
):
    rows, cols, channels = pair.shape
    heads = w_bias.shape[1]
    width = w_out.shape[0]
    keys = residue_mask.shape[0]
    half = cols // 2
    lanes = heads * rows
    me = lax.axis_index("row")
    core = me % 2

    def swap(value, bit):
        return lax.ppermute(value, "row", [(i, i ^ bit) for i in range(row_count)])

    keep, send, bias_copies = pl.pallas_call(
        norm_kernel,
        out_shape=[
            jax.ShapeDtypeStruct((half, rows, channels), BF16),
            jax.ShapeDtypeStruct((half, rows, channels), BF16),
            jax.ShapeDtypeStruct((col_count, rows, heads * cols), BF16),
        ],
        in_specs=[scalars()] + [whole()] * 4,
        out_specs=[whole()] * 3,
    )(core[None], pair, norm_gain[None], norm_shift[None], w_bias)

    bias_row = lax.all_to_all(bias_copies, "col", 0, 0, tiled=True)
    near = jnp.stack([keep, swap(send, 1)])
    near = jnp.concatenate([near, swap(near, 2)])
    near = jnp.concatenate([near, swap(near, 4)])
    far = swap(near, 8)
    chips = row_count // 2
    bias_chunks = jnp.broadcast_to(
        bias_row.reshape(chips, 1, 2, rows, heads * cols),
        (chips, 2, 2, rows, heads * cols),
    ).reshape(row_count, 2, rows, heads * cols)
    bias_here = lax.all_to_all(bias_chunks, "row", 0, 0, tiled=True)

    dead = jnp.broadcast_to(
        jnp.where(residue_mask > 0, 0.0, DEAD).astype(F32)[:, None], (keys, lanes)
    )
    chain_keys = jnp.broadcast_to(chain_index[:, None], (keys, lanes))
    chain_query = lax.dynamic_slice_in_dim(chain_index, (me // 2) * (2 * rows), 2 * rows, 0)
    chain_query = jnp.broadcast_to(
        chain_query.reshape(2, 1, rows), (2, heads, rows)
    ).reshape(1, 2 * lanes)
    wq, wk, wv, wg = (w_proj[:, i * width : (i + 1) * width] for i in range(4))
    keep, send = pl.pallas_call(
        functools.partial(attend_kernel, heads=heads),
        out_shape=[jax.ShapeDtypeStruct((rows, half, channels), BF16)] * 2,
        in_specs=[scalars()] * 2 + [whole()] * 12,
        out_specs=[whole()] * 2,
        scratch_shapes=[
            pltpu.VMEM((half, keys, channels), BF16),
            pltpu.VMEM((keys, 2 * lanes), F32),
            pltpu.VMEM((half, 2 * rows, width), BF16),
        ],
        compiler_params=pltpu.CompilerParams(vmem_limit_bytes=40 * 1024 * 1024),
    )(
        me[None],
        inter_chain,
        near,
        far,
        bias_here,
        dead,
        chain_keys,
        chain_query,
        wk,
        wv.T,
        jnp.concatenate([wq, wg], axis=1),
        gate_shift[None],
        w_out,
        out_shift[None],
    )
    other = swap(send, 1)
    left = jnp.where(core == 0, keep, other)
    right = jnp.where(core == 0, other, keep)
    return jnp.concatenate([left, right], axis=1)


def solution(mesh):
    in_specs = (P("row", "col", None), P(), P(), P(), P(), P(), P(), P(), P(), P(), P())
    out_specs = P("row", "col", None)
    return jax.shard_map(
        functools.partial(on_device, mesh.shape["row"], mesh.shape["col"]),
        mesh=mesh,
        in_specs=in_specs,
        out_specs=out_specs,
        check_vma=False,
    )
```

```python
import functools
import math

import jax
import jax.numpy as jnp
from jax import lax
from jax.experimental import pallas as pl
from jax.experimental.pallas import tpu as pltpu
from jax.sharding import PartitionSpec as P

F32, BF16 = jnp.float32, jnp.bfloat16
NT = (((1,), (1,)), ((), ()))
TN = (((0,), (0,)), ((), ()))
DEAD = -1e30
SPLIT = 4
BUSY = 1_150_000_000
PIECES = (1, 2, 1, 1)
PARAMS = pltpu.CompilerParams(vmem_limit_bytes=32 * 1024 * 1024)


def cost(flops, terms=0, size=1 << 20):
    return pl.CostEstimate(flops=flops, transcendentals=terms, bytes_accessed=size)


def norm_kernel(place_ref, pair_ref, gain_ref, shift_ref, w_bias_ref, *refs):
    part_refs, bias_ref, turned_ref = refs[:SPLIT], refs[SPLIT], refs[SPLIT + 1]
    rows, cols, channels = pair_ref.shape
    heads = w_bias_ref.shape[0]
    copies = bias_ref.shape[0]
    values = pair_ref[...].astype(F32)
    center = jnp.mean(values, axis=-1, keepdims=True)
    away = values - center
    spread = jnp.mean(away * away, axis=-1, keepdims=True)
    normed = away * lax.rsqrt(spread + 1e-05) * gain_ref[...] + shift_ref[...]
    flat = normed.reshape(rows * cols, channels).astype(BF16)
    lanes = heads * cols
    spot = (lax.broadcasted_iota(jnp.int32, (heads, lanes), 1) // cols) == lax.broadcasted_iota(
        jnp.int32, (heads, lanes), 0
    )
    wide = lax.dot_general(
        w_bias_ref[...], spot.astype(F32).astype(BF16), TN, preferred_element_type=F32
    ).astype(BF16)
    every = jnp.dot(flat, wide, preferred_element_type=F32).reshape(rows, cols, lanes)
    own = (lax.broadcasted_iota(jnp.int32, (1, cols, lanes), 2) % cols) == lax.broadcasted_iota(
        jnp.int32, (1, cols, lanes), 1
    )
    bias = jnp.sum(jnp.where(own, every, 0.0), axis=1).astype(BF16)
    bias_ref[...] = jnp.broadcast_to(bias[None], (copies, rows, lanes))
    turned_ref[...] = jnp.swapaxes(normed, 0, 1).astype(BF16)
    quarter = cols // SPLIT
    for step in range(SPLIT):
        source = jnp.bitwise_xor(place_ref[0] % SPLIT, step)
        part_refs[step][...] = turned_ref[pl.ds(source * quarter, quarter)]


def copy_kernel(row_ref, out_ref):
    groups, copies = out_ref.shape[:2]
    for copy in range(copies):
        out_ref[:, copy] = row_ref[...]


def project_kernel(
    place_ref,
    inter_ref,
    *refs,
    size,
):
    x_refs, refs = refs[:SPLIT], refs[SPLIT:]
    wkv_ref, wqg_ref, shift_ref, mask_ref, chain_ref, chain_query_ref, w_out_ref, out_shift_ref = refs[:8]
    key_ref, value_ref, query_ref, gate_ref, side_ref, w_out_copy, out_shift_copy = refs[8:]
    me = place_ref[0]
    cols, rows, channels = x_refs[0].shape[1:]
    width = key_ref.shape[-1]
    scale = 1.0 / math.sqrt(size)
    step = 0
    for x_ref in x_refs:
        for block in range(x_ref.shape[0]):
            x = x_ref[block].reshape(cols * rows, channels)
            both = jnp.dot(x, wkv_ref[...], preferred_element_type=F32).astype(BF16)
            both = both.reshape(cols, rows, 2 * width)
            source = pl.multiple_of(jnp.bitwise_xor(me, step) * rows, rows)
            key_ref[:, pl.ds(source, rows), :] = both[:, :, :width]
            value_ref[:, pl.ds(source, rows), :] = both[:, :, width:]
            step += 1
    for step in range(SPLIT):
        x = x_refs[0][step].reshape(cols * rows, channels)
        both = jnp.dot(x, wqg_ref[...], preferred_element_type=F32)
        query_ref[step] = (both[:, :width] * scale).astype(BF16).reshape(cols, rows, width)
        gate_ref[step] = jax.nn.sigmoid(both[:, width:] + shift_ref[...]).reshape(
            cols, rows, width
        )
    lanes, keys = side_ref.shape[1:]
    lane = lax.broadcasted_iota(jnp.int32, (lanes, keys), 0) // rows
    offset = jnp.zeros((lanes, keys), F32)
    for head in range(width // size):
        offset = jnp.where(lane == head, inter_ref[head], offset)
    dead = jnp.where(mask_ref[...] > 0, 0.0, DEAD)
    chain = chain_ref[...].astype(F32)
    for step in range(SPLIT):
        asked = jnp.broadcast_to(chain_query_ref[step].astype(F32), (lanes, lanes)).T
        asked = jnp.concatenate([asked] * (keys // lanes), axis=1)
        side_ref[step] = jnp.where(chain != asked, offset, 0.0) + dead
    w_out_copy[...] = w_out_ref[...]
    out_shift_copy[...] = out_shift_ref[...]


def attend_kernel(
    place_ref,
    query_ref,
    gate_ref,
    key_ref,
    value_ref,
    bias_ref,
    side_ref,
    w_out_ref,
    out_shift_ref,
    *refs,
    heads,
    first,
):
    out_refs, extra_ref = refs[:-1], refs[-1]
    cols, keys, width = key_ref.shape
    blocks, parts, rows, lanes = bias_ref.shape
    size = width // heads
    me = place_ref[0]
    for b in range(2):
        target = jnp.bitwise_xor(me, first + b) % parts
        bias = bias_ref[:, target].reshape(keys, lanes).astype(F32)
        extra_ref[b * lanes : (b + 1) * lanes, :] = bias.T + side_ref[target]

    query_head = lax.broadcasted_iota(jnp.int32, (1, width), 1) // size
    both_head = (lax.broadcasted_iota(jnp.int32, (1, 2 * width), 1) % width) // size
    ones = jnp.ones((keys, width), BF16)
    gated = []
    for j in range(cols):
        spread = jnp.concatenate(
            [
                jnp.where(query_head == head, query_ref[first + b, j], jnp.zeros((), BF16))
                for b in range(2)
                for head in range(heads)
            ],
            axis=0,
        )
        logits = lax.dot_general(spread, key_ref[j], NT, preferred_element_type=F32)
        logits += extra_ref[...]
        top = jnp.max(logits, axis=1, keepdims=True)
        expo = jnp.exp(logits - top).astype(BF16)
        both = jnp.dot(
            expo, jnp.concatenate([value_ref[j], ones], axis=1), preferred_element_type=F32
        )
        for b in range(2):
            total = None
            for head in range(heads):
                start = (b * heads + head) * rows
                piece = both[start : start + rows]
                total = piece if total is None else jnp.where(both_head == head, piece, total)
            attended = total[:, :width] / total[:, width:]
            gated.append((gate_ref[first + b, j] * attended).astype(BF16))
    update = []
    for b in range(2):
        value = jnp.dot(
            jnp.concatenate(gated[b::2], axis=0), w_out_ref[...], preferred_element_type=F32
        )
        value = (value + out_shift_ref[...]).astype(BF16).reshape(cols, rows, width)
        update += jnp.split(value, PIECES[first + b], axis=0)
    for ref, value in zip(out_refs, update, strict=True):
        ref[...] = value


def place_kernel(place_ref, *refs):
    part_refs, out_ref, turned_ref = list(refs[:-2]), refs[-2], refs[-1]
    quarter = turned_ref.shape[0] // SPLIT
    for step in range(SPLIT):
        start = jnp.bitwise_xor(place_ref[0] % SPLIT, step) * quarter
        count = quarter // PIECES[step]
        for piece in range(PIECES[step]):
            part = part_refs.pop(0)[...].astype(F32)
            turned_ref[pl.ds(start + piece * count, count)] = part
    out_ref[...] = jnp.swapaxes(turned_ref[...], 0, 1).astype(BF16)


def whole():
    return pl.BlockSpec(memory_space=pltpu.VMEM)


def scalars():
    return pl.BlockSpec(memory_space=pltpu.SMEM)


def on_device(
    row_count,
    col_count,
    pair,
    residue_mask,
    chain_index,
    norm_gain,
    norm_shift,
    w_proj,
    gate_shift,
    w_bias,
    inter_chain,
    w_out,
    out_shift,
):
    rows, cols, channels = pair.shape
    heads = w_bias.shape[1]
    width = w_out.shape[0]
    keys = residue_mask.shape[0]
    quarter = cols // SPLIT
    lanes = heads * rows
    me = lax.axis_index("row")
    place = me[None]

    def swap(value, bit):
        return lax.ppermute(value, "row", [(i, i ^ bit) for i in range(row_count)])

    *parts, bias_copies = pl.pallas_call(
        norm_kernel,
        out_shape=[jax.ShapeDtypeStruct((quarter, rows, channels), BF16)] * SPLIT
        + [jax.ShapeDtypeStruct((col_count, rows, heads * cols), BF16)],
        in_specs=[scalars()] + [whole()] * 4,
        out_specs=[whole()] * (SPLIT + 1),
        scratch_shapes=[pltpu.VMEM((cols, rows, channels), BF16)],
        cost_estimate=cost(2 * rows * cols * channels * lanes),
    )(place, pair, norm_gain[None], norm_shift[None], w_bias.T)

    received = [swap(parts[step], step) for step in range(1, SPLIT)]
    near = jnp.stack([parts[0]] + received)
    bias_row = lax.all_to_all(bias_copies, "col", 0, 0, tiled=True)
    gathered = [swap(near, step * SPLIT) for step in range(1, row_count // SPLIT)]

    gate_open = swap(received[-1], 1)
    bias_row, gate_open = lax.optimization_barrier((bias_row, gate_open))
    groups = row_count // SPLIT
    bias_chunks = pl.pallas_call(
        copy_kernel,
        out_shape=jax.ShapeDtypeStruct((groups, SPLIT, SPLIT, rows, lanes), BF16),
        in_specs=[whole()],
        out_specs=whole(),
        compiler_params=PARAMS,
        cost_estimate=cost(0),
    )(bias_row.reshape(groups, SPLIT, rows, lanes)).reshape(row_count, SPLIT, rows, lanes)
    bias_here = lax.all_to_all(bias_chunks, "row", 0, 0, tiled=True)

    wq, wk, wv, wg = (w_proj[:, i * width : (i + 1) * width] for i in range(4))
    chain_query = lax.dynamic_slice_in_dim(
        chain_index, (me // SPLIT) * (SPLIT * rows), SPLIT * rows, 0
    )
    chain_query = jnp.broadcast_to(
        chain_query.reshape(SPLIT, 1, 1, rows), (SPLIT, 1, heads, rows)
    ).reshape(SPLIT, 1, lanes)
    projected = jax.ShapeDtypeStruct((quarter, keys, width), BF16)
    *made, w_out, out_shift = pl.pallas_call(
        functools.partial(project_kernel, size=width // heads),
        out_shape=[projected] * 2
        + [
            jax.ShapeDtypeStruct((SPLIT, quarter, rows, width), BF16),
            jax.ShapeDtypeStruct((SPLIT, quarter, rows, width), F32),
            jax.ShapeDtypeStruct((SPLIT, lanes, keys), F32),
            jax.ShapeDtypeStruct(w_out.shape, BF16),
            jax.ShapeDtypeStruct((1, channels), F32),
        ],
        in_specs=[scalars()] * 2 + [whole()] * 12,
        out_specs=[whole()] * 7,
        compiler_params=PARAMS,
        cost_estimate=cost(20 * BUSY),
    )(
        place,
        inter_chain,
        near,
        *gathered,
        jnp.concatenate([wk, wv], axis=1),
        jnp.concatenate([wq, wg], axis=1),
        gate_shift[None],
        residue_mask[None],
        chain_index[None],
        chain_query,
        w_out,
        out_shift[None],
    )
    key, value, query, gate, side = made

    def attend(first, place):
        return pl.pallas_call(
            functools.partial(attend_kernel, heads=heads, first=first),
            out_shape=[
                jax.ShapeDtypeStruct((quarter // count, rows, channels), BF16)
                for count in PIECES[first : first + 2]
                for _ in range(count)
            ],
            in_specs=[scalars()] + [whole()] * 8,
            out_specs=[whole()] * sum(PIECES[first : first + 2]),
            scratch_shapes=[pltpu.VMEM((2 * lanes, keys), F32)],
            compiler_params=PARAMS,
            cost_estimate=cost(8 * BUSY),
        )(place, query, gate, key, value, bias_here, side, w_out, out_shift)

    two, three = attend(2, place)
    two, three, later = lax.optimization_barrier((two, three, place))
    two, three = swap(two, 2), swap(three, 3)
    own, *one = attend(0, later)
    one = [swap(piece, 1) for piece in one]
    return pl.pallas_call(
        place_kernel,
        out_shape=jax.ShapeDtypeStruct((rows, cols, channels), BF16),
        in_specs=[scalars()] + [whole()] * sum(PIECES),
        out_specs=whole(),
        scratch_shapes=[pltpu.VMEM((cols, rows, channels), F32)],
        compiler_params=PARAMS,
        cost_estimate=cost(0),
    )(place, own, *one, two, three)


def solution(mesh):
    in_specs = (P("row", "col", None), P(), P(), P(), P(), P(), P(), P(), P(), P(), P())
    out_specs = P("row", "col", None)
    return jax.shard_map(
        functools.partial(on_device, mesh.shape["row"], mesh.shape["col"]),
        mesh=mesh,
        in_specs=in_specs,
        out_specs=out_specs,
        check_vma=False,
    )
```

```python
import functools
import math

import jax
import jax.numpy as jnp
from jax import lax
from jax.experimental import pallas as pl
from jax.experimental.pallas import tpu as pltpu
from jax.sharding import PartitionSpec as P

F32, BF16 = jnp.float32, jnp.bfloat16
NT = (((1,), (1,)), ((), ()))
TN = (((0,), (0,)), ((), ()))
DEAD = -1e30
SPLIT = 4
BUSY = 1_150_000_000
PIECES = (1, 2, 1, 1)
PARAMS = pltpu.CompilerParams(vmem_limit_bytes=32 * 1024 * 1024)


def cost(flops, terms=0, size=1 << 20):
    return pl.CostEstimate(flops=flops, transcendentals=terms, bytes_accessed=size)


def norm_kernel(place_ref, pair_ref, gain_ref, shift_ref, w_bias_ref, *refs):
    part_refs, bias_ref, turned_ref = refs[:SPLIT], refs[SPLIT], refs[SPLIT + 1]
    rows, cols, channels = pair_ref.shape
    heads = w_bias_ref.shape[0]
    copies = bias_ref.shape[0]
    values = pair_ref[...].astype(F32)
    center = jnp.mean(values, axis=-1, keepdims=True)
    away = values - center
    spread = jnp.mean(away * away, axis=-1, keepdims=True)
    normed = away * lax.rsqrt(spread + 1e-05) * gain_ref[...] + shift_ref[...]
    flat = normed.reshape(rows * cols, channels).astype(BF16)
    lanes = heads * cols
    spot = (lax.broadcasted_iota(jnp.int32, (heads, lanes), 1) // cols) == lax.broadcasted_iota(
        jnp.int32, (heads, lanes), 0
    )
    wide = lax.dot_general(
        w_bias_ref[...], spot.astype(F32).astype(BF16), TN, preferred_element_type=F32
    ).astype(BF16)
    every = jnp.dot(flat, wide, preferred_element_type=F32).reshape(rows, cols, lanes)
    own = (lax.broadcasted_iota(jnp.int32, (1, cols, lanes), 2) % cols) == lax.broadcasted_iota(
        jnp.int32, (1, cols, lanes), 1
    )
    bias = jnp.sum(jnp.where(own, every, 0.0), axis=1).astype(BF16)
    bias_ref[...] = jnp.broadcast_to(bias[None], (copies, rows, lanes))
    turned_ref[...] = jnp.swapaxes(normed, 0, 1).astype(BF16)
    quarter = cols // SPLIT
    for step in range(SPLIT):
        source = jnp.bitwise_xor(place_ref[0] % SPLIT, step)
        part_refs[step][...] = turned_ref[pl.ds(source * quarter, quarter)]


def copy_kernel(row_ref, out_ref):
    groups, copies = out_ref.shape[:2]
    for copy in range(copies):
        out_ref[:, copy] = row_ref[...]


def gather_kernel(place_ref, *refs):
    x_refs, refs = refs[:SPLIT], refs[SPLIT:]
    count = len(refs) // 2 - 1
    small_refs, all_ref, asked_ref = refs[:count], refs[count], refs[count + 1]
    copy_refs = refs[count + 2 :]
    rows = x_refs[0].shape[2]
    step = 0
    for x_ref in x_refs:
        for block in range(x_ref.shape[0]):
            source = pl.multiple_of(jnp.bitwise_xor(place_ref[0], step) * rows, rows)
            all_ref[:, pl.ds(source, rows), :] = x_ref[block]
            step += 1
    for source, target in zip(small_refs, copy_refs, strict=True):
        target[...] = source[...]
    lanes = asked_ref.shape[-1]
    start = pl.multiple_of(place_ref[0] // SPLIT * (SPLIT * rows), SPLIT * rows)
    asked = small_refs[3][:, pl.ds(start, SPLIT * rows)].astype(F32)
    lane = lax.broadcasted_iota(jnp.int32, (1, lanes), 1) // rows
    for step in range(SPLIT):
        shares = [
            jnp.where(lane == head, asked if head == step else pltpu.roll(asked, rows * (head - step) % lanes, 1), 0.0)
            for head in range(lanes // rows)
        ]
        asked_ref[step] = sum(shares)


def project_kernel(
    place_ref,
    all_ref,
    w_proj_ref,
    shift_ref,
    mask_ref,
    chain_ref,
    inter_ref,
    chain_query_ref,
    key_ref,
    value_ref,
    query_ref,
    gate_ref,
    side_ref,
    *,
    size,
):
    me = place_ref[0]
    cols, rows = query_ref.shape[1:3]
    width = key_ref.shape[-1]
    scale = 1.0 / math.sqrt(size)
    for j in range(cols):
        both = jnp.dot(all_ref[j], w_proj_ref[:, : 2 * width], preferred_element_type=F32)
        key_ref[j] = both[:, :width].astype(BF16)
        value_ref[j] = both[:, width:].astype(BF16)
    for step in range(SPLIT):
        source = pl.multiple_of(jnp.bitwise_xor(me, step) * rows, rows)
        x = all_ref[:, pl.ds(source, rows), :].reshape(cols * rows, width)
        both = jnp.dot(x, w_proj_ref[:, 2 * width :], preferred_element_type=F32)
        query_ref[step] = (both[:, :width] * scale).astype(BF16).reshape(cols, rows, width)
        gate_ref[step] = jax.nn.sigmoid(both[:, width:] + shift_ref[...]).reshape(
            cols, rows, width
        )
    lanes, keys = side_ref.shape[1:]
    lane = lax.broadcasted_iota(jnp.int32, (lanes, keys), 0) // rows
    offset = jnp.zeros((lanes, keys), F32)
    for head in range(width // size):
        offset = jnp.where(lane == head, inter_ref[:, head : head + 1], offset)
    dead = jnp.where(mask_ref[...] > 0, 0.0, DEAD)
    chain = chain_ref[...].astype(F32)
    for step in range(SPLIT):
        asked = jnp.broadcast_to(chain_query_ref[step], (lanes, lanes)).T
        asked = jnp.concatenate([asked] * (keys // lanes), axis=1)
        side_ref[step] = jnp.where(chain != asked, offset, 0.0) + dead


def attend_kernel(
    place_ref,
    query_ref,
    gate_ref,
    key_ref,
    value_ref,
    bias_ref,
    side_ref,
    w_out_ref,
    out_shift_ref,
    *refs,
    heads,
    first,
):
    out_refs, extra_ref = refs[:-1], refs[-1]
    cols, keys, width = key_ref.shape
    blocks, parts, rows, lanes = bias_ref.shape
    size = width // heads
    me = place_ref[0]
    for b in range(2):
        target = jnp.bitwise_xor(me, first + b) % parts
        bias = bias_ref[:, target].reshape(keys, lanes).astype(F32)
        extra_ref[b * lanes : (b + 1) * lanes, :] = bias.T + side_ref[target]

    query_head = lax.broadcasted_iota(jnp.int32, (1, width), 1) // size
    both_head = (lax.broadcasted_iota(jnp.int32, (1, 2 * width), 1) % width) // size
    ones = jnp.ones((keys, width), BF16)
    gated = []
    for j in range(cols):
        spread = jnp.concatenate(
            [
                jnp.where(query_head == head, query_ref[first + b, j], jnp.zeros((), BF16))
                for b in range(2)
                for head in range(heads)
            ],
            axis=0,
        )
        logits = lax.dot_general(spread, key_ref[j], NT, preferred_element_type=F32)
        logits += extra_ref[...]
        top = jnp.max(logits, axis=1, keepdims=True)
        expo = jnp.exp(logits - top).astype(BF16)
        both = jnp.dot(
            expo, jnp.concatenate([value_ref[j], ones], axis=1), preferred_element_type=F32
        )
        for b in range(2):
            total = None
            for head in range(heads):
                start = (b * heads + head) * rows
                piece = both[start : start + rows]
                total = piece if total is None else jnp.where(both_head == head, piece, total)
            attended = total[:, :width] / total[:, width:]
            gated.append((gate_ref[first + b, j] * attended).astype(BF16))
    update = []
    for b in range(2):
        value = jnp.dot(
            jnp.concatenate(gated[b::2], axis=0), w_out_ref[...], preferred_element_type=F32
        )
        value = (value + out_shift_ref[...]).astype(BF16).reshape(cols, rows, width)
        update += jnp.split(value, PIECES[first + b], axis=0)
    for ref, value in zip(out_refs, update, strict=True):
        ref[...] = value


def place_kernel(place_ref, *refs):
    part_refs, out_ref, turned_ref = list(refs[:-2]), refs[-2], refs[-1]
    quarter = turned_ref.shape[0] // SPLIT
    for step in range(SPLIT):
        start = jnp.bitwise_xor(place_ref[0] % SPLIT, step) * quarter
        count = quarter // PIECES[step]
        for piece in range(PIECES[step]):
            part = part_refs.pop(0)[...].astype(F32)
            turned_ref[pl.ds(start + piece * count, count)] = part
    out_ref[...] = jnp.swapaxes(turned_ref[...], 0, 1).astype(BF16)


def whole():
    return pl.BlockSpec(memory_space=pltpu.VMEM)


def scalars():
    return pl.BlockSpec(memory_space=pltpu.SMEM)


def on_device(
    row_count,
    col_count,
    pair,
    residue_mask,
    chain_index,
    norm_gain,
    norm_shift,
    w_proj,
    gate_shift,
    w_bias,
    inter_chain,
    w_out,
    out_shift,
):
    rows, cols, channels = pair.shape
    heads = w_bias.shape[1]
    width = w_out.shape[0]
    keys = residue_mask.shape[0]
    quarter = cols // SPLIT
    lanes = heads * rows
    me = lax.axis_index("row")
    place = me[None]

    def swap(value, bit):
        return lax.ppermute(value, "row", [(i, i ^ bit) for i in range(row_count)])

    *parts, bias_copies = pl.pallas_call(
        norm_kernel,
        out_shape=[jax.ShapeDtypeStruct((quarter, rows, channels), BF16)] * SPLIT
        + [jax.ShapeDtypeStruct((col_count, rows, heads * cols), BF16)],
        in_specs=[scalars()] + [whole()] * 4,
        out_specs=[whole()] * (SPLIT + 1),
        scratch_shapes=[pltpu.VMEM((cols, rows, channels), BF16)],
        cost_estimate=cost(2 * rows * cols * channels * lanes),
    )(place, pair, norm_gain[None], norm_shift[None], w_bias.T)

    received = [swap(parts[step], step) for step in range(1, SPLIT)]
    near = jnp.stack([parts[0]] + received)
    bias_row = lax.all_to_all(bias_copies, "col", 0, 0, tiled=True)
    gathered = [swap(near, step * SPLIT) for step in range(1, row_count // SPLIT)]

    gate_open = swap(received[-1], 1)
    bias_row, gate_open = lax.optimization_barrier((bias_row, gate_open))
    groups = row_count // SPLIT
    bias_chunks = pl.pallas_call(
        copy_kernel,
        out_shape=jax.ShapeDtypeStruct((groups, SPLIT, SPLIT, rows, lanes), BF16),
        in_specs=[whole()],
        out_specs=whole(),
        compiler_params=PARAMS,
        cost_estimate=cost(0),
    )(bias_row.reshape(groups, SPLIT, rows, lanes)).reshape(row_count, SPLIT, rows, lanes)
    bias_here = lax.all_to_all(bias_chunks, "row", 0, 0, tiled=True)

    wq, wk, wv, wg = (w_proj[:, i * width : (i + 1) * width] for i in range(4))
    small = [
        jnp.concatenate([wk, wv, wq, wg], axis=1),
        gate_shift[None],
        residue_mask[None],
        chain_index[None],
        inter_chain[None],
        w_out,
        out_shift[None],
    ]
    everything, chain_query, *small = pl.pallas_call(
        gather_kernel,
        out_shape=[
            jax.ShapeDtypeStruct((quarter, keys, channels), BF16),
            jax.ShapeDtypeStruct((SPLIT, 1, lanes), F32),
        ]
        + [jax.ShapeDtypeStruct(x.shape, x.dtype) for x in small],
        in_specs=[scalars()] + [whole()] * (SPLIT + len(small)),
        out_specs=[whole()] * (2 + len(small)),
        compiler_params=PARAMS,
        cost_estimate=cost(20 * BUSY),
    )(place, near, *gathered, *small)
    everything, bias_here = lax.optimization_barrier((everything, bias_here))
    *small, w_out, out_shift = small
    projected = jax.ShapeDtypeStruct((quarter, keys, width), BF16)
    key, value, query, gate, side = pl.pallas_call(
        functools.partial(project_kernel, size=width // heads),
        out_shape=[
            projected,
            projected,
            jax.ShapeDtypeStruct((SPLIT, quarter, rows, width), BF16),
            jax.ShapeDtypeStruct((SPLIT, quarter, rows, width), F32),
            jax.ShapeDtypeStruct((SPLIT, lanes, keys), F32),
        ],
        in_specs=[scalars()] + [whole()] * 7,
        out_specs=[whole()] * 5,
        compiler_params=PARAMS,
        cost_estimate=cost(2 * BUSY),
    )(place, everything, *small, chain_query)

    def attend(first, place):
        return pl.pallas_call(
            functools.partial(attend_kernel, heads=heads, first=first),
            out_shape=[
                jax.ShapeDtypeStruct((quarter // count, rows, channels), BF16)
                for count in PIECES[first : first + 2]
                for _ in range(count)
            ],
            in_specs=[scalars()] + [whole()] * 8,
            out_specs=[whole()] * sum(PIECES[first : first + 2]),
            scratch_shapes=[pltpu.VMEM((2 * lanes, keys), F32)],
            compiler_params=PARAMS,
            cost_estimate=cost(8 * BUSY),
        )(place, query, gate, key, value, bias_here, side, w_out, out_shift)

    two, three = attend(2, place)
    two, three, later = lax.optimization_barrier((two, three, place))
    two, three = swap(two, 2), swap(three, 3)
    own, *one = attend(0, later)
    one = [swap(piece, 1) for piece in one]
    return pl.pallas_call(
        place_kernel,
        out_shape=jax.ShapeDtypeStruct((rows, cols, channels), BF16),
        in_specs=[scalars()] + [whole()] * sum(PIECES),
        out_specs=whole(),
        scratch_shapes=[pltpu.VMEM((cols, rows, channels), F32)],
        compiler_params=PARAMS,
        cost_estimate=cost(0),
    )(place, own, *one, two, three)


def solution(mesh):
    in_specs = (P("row", "col", None), P(), P(), P(), P(), P(), P(), P(), P(), P(), P())
    out_specs = P("row", "col", None)
    return jax.shard_map(
        functools.partial(on_device, mesh.shape["row"], mesh.shape["col"]),
        mesh=mesh,
        in_specs=in_specs,
        out_specs=out_specs,
        check_vma=False,
    )
```

```python
import functools
import math

import jax
import jax.numpy as jnp
from jax import lax
from jax.experimental import pallas as pl
from jax.experimental.pallas import tpu as pltpu
from jax.sharding import PartitionSpec as P

F32, BF16 = jnp.float32, jnp.bfloat16
NT = (((1,), (1,)), ((), ()))
TN = (((0,), (0,)), ((), ()))
DEAD = -1e30
SPLIT = 4
BUSY = 1_150_000_000
PIECES = (1, 2, 1, 1)
PARAMS = pltpu.CompilerParams(vmem_limit_bytes=32 * 1024 * 1024)


def cost(flops, terms=0, size=1 << 20):
    return pl.CostEstimate(flops=flops, transcendentals=terms, bytes_accessed=size)


def norm_kernel(place_ref, pair_ref, gain_ref, shift_ref, w_bias_ref, *refs):
    keep_ref, near_ref, away_ref, bias_ref, turned_ref = refs
    rows, cols, channels = pair_ref.shape
    heads = w_bias_ref.shape[0]
    copies = bias_ref.shape[0]
    values = pair_ref[...].astype(F32)
    center = jnp.mean(values, axis=-1, keepdims=True)
    away = values - center
    spread = jnp.mean(away * away, axis=-1, keepdims=True)
    normed = away * lax.rsqrt(spread + 1e-05) * gain_ref[...] + shift_ref[...]
    flat = normed.reshape(rows * cols, channels).astype(BF16)
    lanes = heads * cols
    spot = (lax.broadcasted_iota(jnp.int32, (heads, lanes), 1) // cols) == lax.broadcasted_iota(
        jnp.int32, (heads, lanes), 0
    )
    wide = lax.dot_general(
        w_bias_ref[...], spot.astype(F32).astype(BF16), TN, preferred_element_type=F32
    ).astype(BF16)
    every = jnp.dot(flat, wide, preferred_element_type=F32).reshape(rows, cols, lanes)
    own = (lax.broadcasted_iota(jnp.int32, (1, cols, lanes), 2) % cols) == lax.broadcasted_iota(
        jnp.int32, (1, cols, lanes), 1
    )
    bias = jnp.sum(jnp.where(own, every, 0.0), axis=1).astype(BF16)
    bias_ref[...] = jnp.broadcast_to(bias[None], (copies, rows, lanes))
    turned_ref[...] = jnp.swapaxes(normed, 0, 1).astype(BF16)
    quarter = cols // SPLIT
    for step in range(SPLIT):
        source = jnp.bitwise_xor(place_ref[0] % SPLIT, step)
        part = turned_ref[pl.ds(source * quarter, quarter)]
        if step < 2:
            (keep_ref, near_ref)[step][...] = part
        else:
            away_ref[step - 2] = part


def copy_kernel(row_ref, out_ref):
    groups, copies = out_ref.shape[:2]
    for copy in range(copies):
        out_ref[:, copy] = row_ref[...]


def gather_kernel(place_ref, *refs):
    x_refs, refs = refs[:SPLIT], refs[SPLIT:]
    count = (len(refs) - 3) // 2
    small_refs, all_ref, asked_ref, other_ref = refs[:count], *refs[count : count + 3]
    copy_refs = refs[count + 3 :]
    rows = x_refs[0].shape[2]
    for group, x_ref in enumerate(x_refs):
        for block in range(SPLIT):
            source = jnp.bitwise_xor(place_ref[0], group * SPLIT + block) * rows
            all_ref[:, pl.ds(pl.multiple_of(source, rows), rows), :] = x_ref[block]
        other_ref[group] = x_ref[SPLIT - 1]
    for source, target in zip(small_refs, copy_refs, strict=True):
        target[...] = source[...]
    lanes = asked_ref.shape[-1]
    start = pl.multiple_of(place_ref[0] // SPLIT * (SPLIT * rows), SPLIT * rows)
    asked = small_refs[3][:, pl.ds(start, SPLIT * rows)].astype(F32)
    lane = lax.broadcasted_iota(jnp.int32, (1, lanes), 1) // rows
    for step in range(SPLIT):
        shares = [
            jnp.where(lane == head, asked if head == step else pltpu.roll(asked, rows * (head - step) % lanes, 1), 0.0)
            for head in range(lanes // rows)
        ]
        asked_ref[step] = sum(shares)


def project_kernel(
    place_ref,
    all_ref,
    other_ref,
    w_proj_ref,
    shift_ref,
    mask_ref,
    chain_ref,
    inter_ref,
    chain_query_ref,
    key_ref,
    value_ref,
    query_ref,
    gate_ref,
    side_ref,
    *,
    size,
):
    me = place_ref[0]
    cols, rows = query_ref.shape[1:3]
    width = key_ref.shape[-1]
    scale = 1.0 / math.sqrt(size)
    for j in range(cols):
        both = jnp.dot(all_ref[j], w_proj_ref[:, : 2 * width], preferred_element_type=F32)
        key_ref[j] = both[:, :width].astype(BF16)
        value_ref[j] = both[:, width:].astype(BF16)
    for group in range(other_ref.shape[0]):
        x = other_ref[group].reshape(cols * rows, width)
        both = jnp.dot(x, w_proj_ref[:, : 2 * width], preferred_element_type=F32)
        both = both.astype(BF16).reshape(cols, rows, 2 * width)
        source = jnp.bitwise_xor(me, group * SPLIT + SPLIT - 1) * rows
        here = pl.ds(pl.multiple_of(source, rows), rows)
        key_ref[:, here, :] = both[:, :, :width]
        value_ref[:, here, :] = both[:, :, width:]
    for step in range(SPLIT):
        source = pl.multiple_of(jnp.bitwise_xor(me, step) * rows, rows)
        x = all_ref[:, pl.ds(source, rows), :] if step < SPLIT - 1 else other_ref[0]
        x = x.reshape(cols * rows, width)
        both = jnp.dot(x, w_proj_ref[:, 2 * width :], preferred_element_type=F32)
        query_ref[step] = (both[:, :width] * scale).astype(BF16).reshape(cols, rows, width)
        gate_ref[step] = jax.nn.sigmoid(both[:, width:] + shift_ref[...]).reshape(
            cols, rows, width
        )
    lanes, keys = side_ref.shape[1:]
    lane = lax.broadcasted_iota(jnp.int32, (lanes, keys), 0) // rows
    offset = jnp.zeros((lanes, keys), F32)
    for head in range(width // size):
        offset = jnp.where(lane == head, inter_ref[:, head : head + 1], offset)
    dead = jnp.where(mask_ref[...] > 0, 0.0, DEAD)
    chain = chain_ref[...].astype(F32)
    for step in range(SPLIT):
        asked = jnp.broadcast_to(chain_query_ref[step], (lanes, lanes)).T
        asked = jnp.concatenate([asked] * (keys // lanes), axis=1)
        side_ref[step] = jnp.where(chain != asked, offset, 0.0) + dead


def attend_kernel(
    place_ref,
    query_ref,
    gate_ref,
    key_ref,
    value_ref,
    bias_ref,
    side_ref,
    w_out_ref,
    out_shift_ref,
    *refs,
    heads,
    first,
):
    out_refs, extra_ref = refs[:-1], refs[-1]
    cols, keys, width = key_ref.shape
    blocks, parts, rows, lanes = bias_ref.shape
    size = width // heads
    me = place_ref[0]
    for b in range(2):
        target = jnp.bitwise_xor(me, first + b) % parts
        bias = bias_ref[:, target].reshape(keys, lanes).astype(F32)
        extra_ref[b * lanes : (b + 1) * lanes, :] = bias.T + side_ref[target]

    query_head = lax.broadcasted_iota(jnp.int32, (1, width), 1) // size
    both_head = (lax.broadcasted_iota(jnp.int32, (1, 2 * width), 1) % width) // size
    ones = jnp.ones((keys, width), BF16)
    gated = []
    for j in range(cols):
        spread = jnp.concatenate(
            [
                jnp.where(query_head == head, query_ref[first + b, j], jnp.zeros((), BF16))
                for b in range(2)
                for head in range(heads)
            ],
            axis=0,
        )
        logits = lax.dot_general(spread, key_ref[j], NT, preferred_element_type=F32)
        logits += extra_ref[...]
        top = jnp.max(logits, axis=1, keepdims=True)
        expo = jnp.exp(logits - top).astype(BF16)
        both = jnp.dot(
            expo, jnp.concatenate([value_ref[j], ones], axis=1), preferred_element_type=F32
        )
        for b in range(2):
            total = None
            for head in range(heads):
                start = (b * heads + head) * rows
                piece = both[start : start + rows]
                total = piece if total is None else jnp.where(both_head == head, piece, total)
            attended = total[:, :width] / total[:, width:]
            gated.append((gate_ref[first + b, j] * attended).astype(BF16))
    update = []
    for b in range(2):
        value = jnp.dot(
            jnp.concatenate(gated[b::2], axis=0), w_out_ref[...], preferred_element_type=F32
        )
        value = (value + out_shift_ref[...]).astype(BF16).reshape(cols, rows, width)
        update += jnp.split(value, PIECES[first + b], axis=0)
    for ref, value in zip(out_refs, update, strict=True):
        ref[...] = value


def place_kernel(place_ref, *refs):
    part_refs, out_ref, turned_ref = list(refs[:-2]), refs[-2], refs[-1]
    quarter = turned_ref.shape[0] // SPLIT
    for step in range(SPLIT):
        start = jnp.bitwise_xor(place_ref[0] % SPLIT, step) * quarter
        count = quarter // PIECES[step]
        for piece in range(PIECES[step]):
            part = part_refs.pop(0)[...].astype(F32)
            turned_ref[pl.ds(start + piece * count, count)] = part
    out_ref[...] = jnp.swapaxes(turned_ref[...], 0, 1).astype(BF16)


def whole():
    return pl.BlockSpec(memory_space=pltpu.VMEM)


def scalars():
    return pl.BlockSpec(memory_space=pltpu.SMEM)


def on_device(
    row_count,
    col_count,
    pair,
    residue_mask,
    chain_index,
    norm_gain,
    norm_shift,
    w_proj,
    gate_shift,
    w_bias,
    inter_chain,
    w_out,
    out_shift,
):
    rows, cols, channels = pair.shape
    heads = w_bias.shape[1]
    width = w_out.shape[0]
    keys = residue_mask.shape[0]
    quarter = cols // SPLIT
    lanes = heads * rows
    me = lax.axis_index("row")
    place = me[None]

    def swap(value, bit):
        return lax.ppermute(value, "row", [(i, i ^ bit) for i in range(row_count)])

    part = jax.ShapeDtypeStruct((quarter, rows, channels), BF16)
    keep, near, away, bias_copies = pl.pallas_call(
        norm_kernel,
        out_shape=[
            part,
            part,
            jax.ShapeDtypeStruct((2, quarter, rows, channels), BF16),
            jax.ShapeDtypeStruct((col_count, rows, heads * cols), BF16),
        ],
        in_specs=[scalars()] + [whole()] * 4,
        out_specs=[whole()] * 4,
        scratch_shapes=[pltpu.VMEM((cols, rows, channels), BF16)],
        cost_estimate=cost(2 * rows * cols * channels * lanes),
    )(place, pair, norm_gain[None], norm_shift[None], w_bias.T)

    passed, away = swap(near, 1), swap(away, 2)
    near = jnp.concatenate([keep[None], passed[None], away])
    bias_row = lax.all_to_all(bias_copies, "col", 0, 0, tiled=True)
    gathered = [swap(near, step * SPLIT) for step in range(1, row_count // SPLIT)]

    gate_open = swap(passed, 1)
    bias_row, gate_open = lax.optimization_barrier((bias_row, gate_open))
    groups = row_count // SPLIT
    bias_chunks = pl.pallas_call(
        copy_kernel,
        out_shape=jax.ShapeDtypeStruct((groups, SPLIT, SPLIT, rows, lanes), BF16),
        in_specs=[whole()],
        out_specs=whole(),
        compiler_params=PARAMS,
        cost_estimate=cost(0),
    )(bias_row.reshape(groups, SPLIT, rows, lanes)).reshape(row_count, SPLIT, rows, lanes)
    bias_here = lax.all_to_all(bias_chunks, "row", 0, 0, tiled=True)

    wq, wk, wv, wg = (w_proj[:, i * width : (i + 1) * width] for i in range(4))
    small = [
        jnp.concatenate([wk, wv, wq, wg], axis=1),
        gate_shift[None],
        residue_mask[None],
        chain_index[None],
        inter_chain[None],
        w_out,
        out_shift[None],
    ]
    everything, chain_query, other, *small = pl.pallas_call(
        gather_kernel,
        out_shape=[
            jax.ShapeDtypeStruct((quarter, keys, channels), BF16),
            jax.ShapeDtypeStruct((SPLIT, 1, lanes), F32),
            jax.ShapeDtypeStruct((row_count // SPLIT, quarter, rows, channels), BF16),
        ]
        + [jax.ShapeDtypeStruct(x.shape, x.dtype) for x in small],
        in_specs=[scalars()] + [whole()] * (SPLIT + len(small)),
        out_specs=[whole()] * (3 + len(small)),
        compiler_params=PARAMS,
        cost_estimate=cost(20 * BUSY),
    )(place, near, *gathered, *small)
    other = swap(other, 1)
    everything, other, bias_here = lax.optimization_barrier((everything, other, bias_here))
    *small, w_out, out_shift = small
    projected = jax.ShapeDtypeStruct((quarter, keys, width), BF16)
    key, value, query, gate, side = pl.pallas_call(
        functools.partial(project_kernel, size=width // heads),
        out_shape=[
            projected,
            projected,
            jax.ShapeDtypeStruct((SPLIT, quarter, rows, width), BF16),
            jax.ShapeDtypeStruct((SPLIT, quarter, rows, width), F32),
            jax.ShapeDtypeStruct((SPLIT, lanes, keys), F32),
        ],
        in_specs=[scalars()] + [whole()] * 8,
        out_specs=[whole()] * 5,
        compiler_params=PARAMS,
        cost_estimate=cost(2 * BUSY),
    )(place, everything, other, *small, chain_query)

    def attend(first, place):
        return pl.pallas_call(
            functools.partial(attend_kernel, heads=heads, first=first),
            out_shape=[
                jax.ShapeDtypeStruct((quarter // count, rows, channels), BF16)
                for count in PIECES[first : first + 2]
                for _ in range(count)
            ],
            in_specs=[scalars()] + [whole()] * 8,
            out_specs=[whole()] * sum(PIECES[first : first + 2]),
            scratch_shapes=[pltpu.VMEM((2 * lanes, keys), F32)],
            compiler_params=PARAMS,
            cost_estimate=cost(8 * BUSY),
        )(place, query, gate, key, value, bias_here, side, w_out, out_shift)

    two, three = attend(2, place)
    two, three, later = lax.optimization_barrier((two, three, place))
    two, three = swap(two, 2), swap(three, 3)
    own, *one = attend(0, later)
    one = [swap(piece, 1) for piece in one]
    return pl.pallas_call(
        place_kernel,
        out_shape=jax.ShapeDtypeStruct((rows, cols, channels), BF16),
        in_specs=[scalars()] + [whole()] * sum(PIECES),
        out_specs=whole(),
        scratch_shapes=[pltpu.VMEM((cols, rows, channels), F32)],
        compiler_params=PARAMS,
        cost_estimate=cost(0),
    )(place, own, *one, two, three)


def solution(mesh):
    in_specs = (P("row", "col", None), P(), P(), P(), P(), P(), P(), P(), P(), P(), P())
    out_specs = P("row", "col", None)
    return jax.shard_map(
        functools.partial(on_device, mesh.shape["row"], mesh.shape["col"]),
        mesh=mesh,
        in_specs=in_specs,
        out_specs=out_specs,
        check_vma=False,
    )
```

```python
import functools
import math

import jax
import jax.numpy as jnp
from jax import lax
from jax.experimental import pallas as pl
from jax.experimental.pallas import tpu as pltpu
from jax.sharding import PartitionSpec as P

F32, BF16 = jnp.float32, jnp.bfloat16
NT = (((1,), (1,)), ((), ()))
TN = (((0,), (0,)), ((), ()))
DEAD = -1e30
SPLIT = 4
BUSY = 1_150_000_000
PIECES = (1, 2, 1, 1)
PARAMS = pltpu.CompilerParams(vmem_limit_bytes=32 * 1024 * 1024)


def cost(flops, terms=0, size=1 << 20):
    return pl.CostEstimate(flops=flops, transcendentals=terms, bytes_accessed=size)


def norm_kernel(place_ref, pair_ref, gain_ref, shift_ref, w_bias_ref, *refs):
    keep_ref, near_ref, away_ref, bias_ref, turned_ref = refs
    rows, cols, channels = pair_ref.shape
    heads = w_bias_ref.shape[0]
    copies = bias_ref.shape[0]
    values = pair_ref[...].astype(F32)
    center = jnp.mean(values, axis=-1, keepdims=True)
    away = values - center
    spread = jnp.mean(away * away, axis=-1, keepdims=True)
    normed = away * lax.rsqrt(spread + 1e-05) * gain_ref[...] + shift_ref[...]
    flat = normed.reshape(rows * cols, channels).astype(BF16)
    lanes = heads * cols
    spot = (lax.broadcasted_iota(jnp.int32, (heads, lanes), 1) // cols) == lax.broadcasted_iota(
        jnp.int32, (heads, lanes), 0
    )
    wide = lax.dot_general(
        w_bias_ref[...], spot.astype(F32).astype(BF16), TN, preferred_element_type=F32
    ).astype(BF16)
    every = jnp.dot(flat, wide, preferred_element_type=F32).reshape(rows, cols, lanes)
    own = (lax.broadcasted_iota(jnp.int32, (1, cols, lanes), 2) % cols) == lax.broadcasted_iota(
        jnp.int32, (1, cols, lanes), 1
    )
    bias = jnp.sum(jnp.where(own, every, 0.0), axis=1).astype(BF16)
    bias_ref[...] = jnp.broadcast_to(bias[None], (copies, rows, lanes))
    turned_ref[...] = jnp.swapaxes(normed, 0, 1).astype(BF16)
    quarter = cols // SPLIT
    for step in range(SPLIT):
        source = jnp.bitwise_xor(place_ref[0] % SPLIT, step)
        part = turned_ref[pl.ds(source * quarter, quarter)]
        if step < 2:
            (keep_ref, near_ref)[step][...] = part
        else:
            away_ref[step - 2] = part


def copy_kernel(row_ref, out_ref):
    for copy in range(2):
        for core in range(2):
            out_ref[:, copy, core] = row_ref[:, :, core]


def gather_kernel(place_ref, *refs):
    x_refs, refs = refs[:SPLIT], refs[SPLIT:]
    count = (len(refs) - 3) // 2
    small_refs, all_ref, asked_ref, other_ref = refs[:count], *refs[count : count + 3]
    copy_refs = refs[count + 3 :]
    rows = x_refs[0].shape[2]
    for group, x_ref in enumerate(x_refs):
        for block in range(SPLIT):
            source = jnp.bitwise_xor(place_ref[0], group * SPLIT + block) * rows
            all_ref[:, pl.ds(pl.multiple_of(source, rows), rows), :] = x_ref[block]
        other_ref[group] = x_ref[SPLIT - 1]
    for source, target in zip(small_refs, copy_refs, strict=True):
        target[...] = source[...]
    lanes = asked_ref.shape[-1]
    start = pl.multiple_of(place_ref[0] // SPLIT * (SPLIT * rows), SPLIT * rows)
    asked = small_refs[3][:, pl.ds(start, SPLIT * rows)].astype(F32)
    lane = lax.broadcasted_iota(jnp.int32, (1, lanes), 1) // rows
    for step in range(SPLIT):
        shares = [
            jnp.where(lane == head, asked if head == step else pltpu.roll(asked, rows * (head - step) % lanes, 1), 0.0)
            for head in range(lanes // rows)
        ]
        asked_ref[step] = sum(shares)


def project_kernel(
    place_ref,
    all_ref,
    other_ref,
    w_proj_ref,
    shift_ref,
    mask_ref,
    chain_ref,
    inter_ref,
    chain_query_ref,
    key_ref,
    value_ref,
    query_ref,
    gate_ref,
    side_ref,
    *,
    size,
):
    me = place_ref[0]
    cols, rows = query_ref.shape[1:3]
    width = key_ref.shape[-1]
    scale = 1.0 / math.sqrt(size)
    for j in range(cols):
        both = jnp.dot(all_ref[j], w_proj_ref[:, : 2 * width], preferred_element_type=F32)
        key_ref[j] = both[:, :width].astype(BF16)
        value_ref[j] = both[:, width:].astype(BF16)
    for group in range(other_ref.shape[0]):
        x = other_ref[group].reshape(cols * rows, width)
        both = jnp.dot(x, w_proj_ref[:, : 2 * width], preferred_element_type=F32)
        both = both.astype(BF16).reshape(cols, rows, 2 * width)
        source = jnp.bitwise_xor(me, group * SPLIT + SPLIT - 1) * rows
        here = pl.ds(pl.multiple_of(source, rows), rows)
        key_ref[:, here, :] = both[:, :, :width]
        value_ref[:, here, :] = both[:, :, width:]
    for step in range(SPLIT):
        source = pl.multiple_of(jnp.bitwise_xor(me, step) * rows, rows)
        x = all_ref[:, pl.ds(source, rows), :] if step < SPLIT - 1 else other_ref[0]
        x = x.reshape(cols * rows, width)
        both = jnp.dot(x, w_proj_ref[:, 2 * width :], preferred_element_type=F32)
        query_ref[step] = (both[:, :width] * scale).astype(BF16).reshape(cols, rows, width)
        gate_ref[step] = jax.nn.sigmoid(both[:, width:] + shift_ref[...]).reshape(
            cols, rows, width
        )
    lanes, keys = side_ref.shape[1:]
    lane = lax.broadcasted_iota(jnp.int32, (lanes, keys), 0) // rows
    offset = jnp.zeros((lanes, keys), F32)
    for head in range(width // size):
        offset = jnp.where(lane == head, inter_ref[:, head : head + 1], offset)
    dead = jnp.where(mask_ref[...] > 0, 0.0, DEAD)
    chain = chain_ref[...].astype(F32)
    for step in range(SPLIT):
        asked = jnp.broadcast_to(chain_query_ref[step], (lanes, lanes)).T
        asked = jnp.concatenate([asked] * (keys // lanes), axis=1)
        side_ref[step] = jnp.where(chain != asked, offset, 0.0) + dead


def attend_kernel(
    place_ref,
    query_ref,
    gate_ref,
    key_ref,
    value_ref,
    bias_ref,
    other_bias_ref,
    side_ref,
    w_out_ref,
    out_shift_ref,
    *refs,
    heads,
    first,
):
    out_refs, extra_ref = refs[:-1], refs[-1]
    cols, keys, width = key_ref.shape
    rows, lanes = bias_ref.shape[2:]
    size = width // heads
    me = place_ref[0]
    for b in range(2):
        target = jnp.bitwise_xor(me, first + b) % SPLIT
        source = (bias_ref, other_bias_ref)[(first + b) % 2]
        bias = source[:, target // 2].reshape(keys, lanes).astype(F32)
        extra_ref[b * lanes : (b + 1) * lanes, :] = bias.T + side_ref[target]

    query_head = lax.broadcasted_iota(jnp.int32, (1, width), 1) // size
    both_head = (lax.broadcasted_iota(jnp.int32, (1, 2 * width), 1) % width) // size
    ones = jnp.ones((keys, width), BF16)
    gated = []
    for j in range(cols):
        spread = jnp.concatenate(
            [
                jnp.where(query_head == head, query_ref[first + b, j], jnp.zeros((), BF16))
                for b in range(2)
                for head in range(heads)
            ],
            axis=0,
        )
        logits = lax.dot_general(spread, key_ref[j], NT, preferred_element_type=F32)
        logits += extra_ref[...]
        top = jnp.max(logits, axis=1, keepdims=True)
        expo = jnp.exp(logits - top).astype(BF16)
        both = jnp.dot(
            expo, jnp.concatenate([value_ref[j], ones], axis=1), preferred_element_type=F32
        )
        for b in range(2):
            total = None
            for head in range(heads):
                start = (b * heads + head) * rows
                piece = both[start : start + rows]
                total = piece if total is None else jnp.where(both_head == head, piece, total)
            attended = total[:, :width] / total[:, width:]
            gated.append((gate_ref[first + b, j] * attended).astype(BF16))
    update = []
    for b in range(2):
        value = jnp.dot(
            jnp.concatenate(gated[b::2], axis=0), w_out_ref[...], preferred_element_type=F32
        )
        value = (value + out_shift_ref[...]).astype(BF16).reshape(cols, rows, width)
        update += jnp.split(value, PIECES[first + b], axis=0)
    for ref, value in zip(out_refs, update, strict=True):
        ref[...] = value


def place_kernel(place_ref, *refs):
    part_refs, out_ref, turned_ref = list(refs[:-2]), refs[-2], refs[-1]
    quarter = turned_ref.shape[0] // SPLIT
    for step in range(SPLIT):
        start = jnp.bitwise_xor(place_ref[0] % SPLIT, step) * quarter
        count = quarter // PIECES[step]
        for piece in range(PIECES[step]):
            part = part_refs.pop(0)[...].astype(F32)
            turned_ref[pl.ds(start + piece * count, count)] = part
    out_ref[...] = jnp.swapaxes(turned_ref[...], 0, 1).astype(BF16)


def whole():
    return pl.BlockSpec(memory_space=pltpu.VMEM)


def scalars():
    return pl.BlockSpec(memory_space=pltpu.SMEM)


def on_device(
    row_count,
    col_count,
    pair,
    residue_mask,
    chain_index,
    norm_gain,
    norm_shift,
    w_proj,
    gate_shift,
    w_bias,
    inter_chain,
    w_out,
    out_shift,
):
    rows, cols, channels = pair.shape
    heads = w_bias.shape[1]
    width = w_out.shape[0]
    keys = residue_mask.shape[0]
    quarter = cols // SPLIT
    lanes = heads * rows
    me = lax.axis_index("row")
    place = me[None]

    def swap(value, bit):
        return lax.ppermute(value, "row", [(i, i ^ bit) for i in range(row_count)])

    part = jax.ShapeDtypeStruct((quarter, rows, channels), BF16)
    keep, near, away, bias_copies = pl.pallas_call(
        norm_kernel,
        out_shape=[
            part,
            part,
            jax.ShapeDtypeStruct((2, quarter, rows, channels), BF16),
            jax.ShapeDtypeStruct((col_count, rows, heads * cols), BF16),
        ],
        in_specs=[scalars()] + [whole()] * 4,
        out_specs=[whole()] * 4,
        scratch_shapes=[pltpu.VMEM((cols, rows, channels), BF16)],
        cost_estimate=cost(2 * rows * cols * channels * lanes),
    )(place, pair, norm_gain[None], norm_shift[None], w_bias.T)

    passed, away = swap(near, 1), swap(away, 2)
    near = jnp.concatenate([keep[None], passed[None], away])
    bias_row = lax.all_to_all(bias_copies, "col", 0, 0, tiled=True)
    gathered = [swap(near, step * SPLIT) for step in range(1, row_count // SPLIT)]

    gate_open = swap(passed, 1)
    bias_row, gate_open = lax.optimization_barrier((bias_row, gate_open))
    groups = row_count // SPLIT
    bias_chunks = pl.pallas_call(
        copy_kernel,
        out_shape=jax.ShapeDtypeStruct((groups, 2, 2, 2, rows, lanes), BF16),
        in_specs=[whole()],
        out_specs=whole(),
        compiler_params=PARAMS,
        cost_estimate=cost(0),
    )(bias_row.reshape(groups, 2, 2, rows, lanes)).reshape(row_count, 2, rows, lanes)
    bias_here = lax.all_to_all(bias_chunks, "row", 0, 0, tiled=True)

    wq, wk, wv, wg = (w_proj[:, i * width : (i + 1) * width] for i in range(4))
    small = [
        jnp.concatenate([wk, wv, wq, wg], axis=1),
        gate_shift[None],
        residue_mask[None],
        chain_index[None],
        inter_chain[None],
        w_out,
        out_shift[None],
    ]
    everything, chain_query, other, *small = pl.pallas_call(
        gather_kernel,
        out_shape=[
            jax.ShapeDtypeStruct((quarter, keys, channels), BF16),
            jax.ShapeDtypeStruct((SPLIT, 1, lanes), F32),
            jax.ShapeDtypeStruct((row_count // SPLIT, quarter, rows, channels), BF16),
        ]
        + [jax.ShapeDtypeStruct(x.shape, x.dtype) for x in small],
        in_specs=[scalars()] + [whole()] * (SPLIT + len(small)),
        out_specs=[whole()] * (3 + len(small)),
        compiler_params=PARAMS,
        cost_estimate=cost(20 * BUSY),
    )(place, near, *gathered, *small)
    other = swap(other, 1)
    everything, bias_here = lax.optimization_barrier((everything, bias_here))
    bias_there = swap(bias_here, 1)
    *small, w_out, out_shift = small
    projected = jax.ShapeDtypeStruct((quarter, keys, width), BF16)
    key, value, query, gate, side = pl.pallas_call(
        functools.partial(project_kernel, size=width // heads),
        out_shape=[
            projected,
            projected,
            jax.ShapeDtypeStruct((SPLIT, quarter, rows, width), BF16),
            jax.ShapeDtypeStruct((SPLIT, quarter, rows, width), F32),
            jax.ShapeDtypeStruct((SPLIT, lanes, keys), F32),
        ],
        in_specs=[scalars()] + [whole()] * 8,
        out_specs=[whole()] * 5,
        compiler_params=PARAMS,
        cost_estimate=cost(2 * BUSY),
    )(place, everything, other, *small, chain_query)

    def attend(first, place):
        return pl.pallas_call(
            functools.partial(attend_kernel, heads=heads, first=first),
            out_shape=[
                jax.ShapeDtypeStruct((quarter // count, rows, channels), BF16)
                for count in PIECES[first : first + 2]
                for _ in range(count)
            ],
            in_specs=[scalars()] + [whole()] * 9,
            out_specs=[whole()] * sum(PIECES[first : first + 2]),
            scratch_shapes=[pltpu.VMEM((2 * lanes, keys), F32)],
            compiler_params=PARAMS,
            cost_estimate=cost(8 * BUSY),
        )(place, query, gate, key, value, bias_here, bias_there, side, w_out, out_shift)

    two, three = attend(2, place)
    two, three, later = lax.optimization_barrier((two, three, place))
    two, three = swap(two, 2), swap(three, 3)
    own, *one = attend(0, later)
    one = [swap(piece, 1) for piece in one]
    return pl.pallas_call(
        place_kernel,
        out_shape=jax.ShapeDtypeStruct((rows, cols, channels), BF16),
        in_specs=[scalars()] + [whole()] * sum(PIECES),
        out_specs=whole(),
        scratch_shapes=[pltpu.VMEM((cols, rows, channels), F32)],
        compiler_params=PARAMS,
        cost_estimate=cost(0),
    )(place, own, *one, two, three)


def solution(mesh):
    in_specs = (P("row", "col", None), P(), P(), P(), P(), P(), P(), P(), P(), P(), P())
    out_specs = P("row", "col", None)
    return jax.shard_map(
        functools.partial(on_device, mesh.shape["row"], mesh.shape["col"]),
        mesh=mesh,
        in_specs=in_specs,
        out_specs=out_specs,
        check_vma=False,
    )
```

```python
import functools
import math

import jax
import jax.numpy as jnp
from jax import lax
from jax.experimental import pallas as pl
from jax.experimental.pallas import tpu as pltpu
from jax.sharding import PartitionSpec as P

F32, BF16 = jnp.float32, jnp.bfloat16
NT = (((1,), (1,)), ((), ()))
TN = (((0,), (0,)), ((), ()))
DEAD = -1e30
SPLIT = 4
BUSY = 1_150_000_000
PIECES = (1, 2, 1, 1)
PARAMS = pltpu.CompilerParams(vmem_limit_bytes=32 * 1024 * 1024)


def cost(flops, terms=0, size=1 << 20):
    return pl.CostEstimate(flops=flops, transcendentals=terms, bytes_accessed=size)


def norm_kernel(place_ref, pair_ref, gain_ref, shift_ref, w_bias_ref, *refs):
    mine_ref, away_ref, bias_ref, turned_ref = refs
    rows, cols, channels = pair_ref.shape
    heads = w_bias_ref.shape[0]
    copies = bias_ref.shape[0]
    values = pair_ref[...].astype(F32)
    center = jnp.mean(values, axis=-1, keepdims=True)
    away = values - center
    spread = jnp.mean(away * away, axis=-1, keepdims=True)
    normed = away * lax.rsqrt(spread + 1e-05) * gain_ref[...] + shift_ref[...]
    flat = normed.reshape(rows * cols, channels).astype(BF16)
    lanes = heads * cols
    spot = (lax.broadcasted_iota(jnp.int32, (heads, lanes), 1) // cols) == lax.broadcasted_iota(
        jnp.int32, (heads, lanes), 0
    )
    wide = lax.dot_general(
        w_bias_ref[...], spot.astype(F32).astype(BF16), TN, preferred_element_type=F32
    ).astype(BF16)
    every = jnp.dot(flat, wide, preferred_element_type=F32).reshape(rows, cols, lanes)
    own = (lax.broadcasted_iota(jnp.int32, (1, cols, lanes), 2) % cols) == lax.broadcasted_iota(
        jnp.int32, (1, cols, lanes), 1
    )
    bias = jnp.sum(jnp.where(own, every, 0.0), axis=1).astype(BF16)
    bias_ref[...] = jnp.broadcast_to(bias[None], (copies, rows, lanes))
    turned_ref[...] = jnp.swapaxes(normed, 0, 1).astype(BF16)
    quarter = cols // SPLIT
    for step in range(SPLIT):
        source = jnp.bitwise_xor(place_ref[0] % SPLIT, step)
        target = (mine_ref, away_ref)[step // 2]
        target[step % 2] = turned_ref[pl.ds(source * quarter, quarter)]


def copy_kernel(row_ref, out_ref):
    for copy in range(2):
        for core in range(2):
            out_ref[:, copy, core] = row_ref[:, :, core]


def gather_kernel(place_ref, *refs):
    x_refs, refs = refs[:SPLIT], refs[SPLIT:]
    count = (len(refs) - 4) // 2
    small_refs, all_ref, asked_ref = refs[:count], *refs[count : count + 2]
    other_refs, copy_refs = refs[count + 2 : count + 4], refs[count + 4 :]
    rows = x_refs[0].shape[2]
    for group, x_ref in enumerate(x_refs):
        for half in range(2):
            all_ref[group, half] = x_ref[2 * half]
            other_refs[half][group] = x_ref[2 * half + 1]
    for source, target in zip(small_refs, copy_refs, strict=True):
        target[...] = source[...]
    lanes = asked_ref.shape[-1]
    start = pl.multiple_of(place_ref[0] // SPLIT * (SPLIT * rows), SPLIT * rows)
    asked = small_refs[3][:, pl.ds(start, SPLIT * rows)].astype(F32)
    lane = lax.broadcasted_iota(jnp.int32, (1, lanes), 1) // rows
    for step in range(SPLIT):
        shares = [
            jnp.where(lane == head, asked if head == step else pltpu.roll(asked, rows * (head - step) % lanes, 1), 0.0)
            for head in range(lanes // rows)
        ]
        asked_ref[step] = sum(shares)


def project_kernel(
    place_ref,
    all_ref,
    other_ref,
    rest_ref,
    w_proj_ref,
    shift_ref,
    mask_ref,
    chain_ref,
    inter_ref,
    chain_query_ref,
    key_ref,
    value_ref,
    query_ref,
    gate_ref,
    side_ref,
    *,
    size,
):
    me = place_ref[0]
    cols, rows = query_ref.shape[1:3]
    width = key_ref.shape[-1]
    scale = 1.0 / math.sqrt(size)
    others = other_ref, rest_ref
    for core in range(2):
        for group in range(all_ref.shape[0]):
            for half in range(2):
                x = others[half][group] if core else all_ref[group, half]
                x = x.reshape(cols * rows, width)
                both = jnp.dot(x, w_proj_ref[:, : 2 * width], preferred_element_type=F32)
                both = both.astype(BF16).reshape(cols, rows, 2 * width)
                source = jnp.bitwise_xor(me, group * SPLIT + 2 * half + core) * rows
                here = pl.ds(pl.multiple_of(source, rows), rows)
                key_ref[:, here, :] = both[:, :, :width]
                value_ref[:, here, :] = both[:, :, width:]
    for step in range(SPLIT):
        x = others[step // 2][0] if step % 2 else all_ref[0, step // 2]
        x = x.reshape(cols * rows, width)
        both = jnp.dot(x, w_proj_ref[:, 2 * width :], preferred_element_type=F32)
        query_ref[step] = (both[:, :width] * scale).astype(BF16).reshape(cols, rows, width)
        gate_ref[step] = jax.nn.sigmoid(both[:, width:] + shift_ref[...]).reshape(
            cols, rows, width
        )
    lanes, keys = side_ref.shape[1:]
    lane = lax.broadcasted_iota(jnp.int32, (lanes, keys), 0) // rows
    offset = jnp.zeros((lanes, keys), F32)
    for head in range(width // size):
        offset = jnp.where(lane == head, inter_ref[:, head : head + 1], offset)
    dead = jnp.where(mask_ref[...] > 0, 0.0, DEAD)
    chain = chain_ref[...].astype(F32)
    for step in range(SPLIT):
        asked = jnp.broadcast_to(chain_query_ref[step], (lanes, lanes)).T
        asked = jnp.concatenate([asked] * (keys // lanes), axis=1)
        side_ref[step] = jnp.where(chain != asked, offset, 0.0) + dead


def attend_kernel(
    place_ref,
    query_ref,
    gate_ref,
    key_ref,
    value_ref,
    bias_ref,
    other_bias_ref,
    side_ref,
    w_out_ref,
    out_shift_ref,
    *refs,
    heads,
    first,
    count,
):
    out_refs, extra_ref = refs[:-1], refs[-1]
    cols, keys, width = key_ref.shape
    rows, lanes = bias_ref.shape[2:]
    size = width // heads
    me = place_ref[0]
    for b in range(count):
        target = jnp.bitwise_xor(me, first + b) % SPLIT
        source = (bias_ref, other_bias_ref)[(first + b) % 2]
        bias = source[:, target // 2].reshape(keys, lanes).astype(F32)
        extra_ref[b * lanes : (b + 1) * lanes, :] = bias.T + side_ref[target]

    query_head = lax.broadcasted_iota(jnp.int32, (1, width), 1) // size
    both_head = (lax.broadcasted_iota(jnp.int32, (1, 2 * width), 1) % width) // size
    ones = jnp.ones((keys, width), BF16)
    gated = []
    for j in range(cols):
        spread = jnp.concatenate(
            [
                jnp.where(query_head == head, query_ref[first + b, j], jnp.zeros((), BF16))
                for b in range(count)
                for head in range(heads)
            ],
            axis=0,
        )
        logits = lax.dot_general(spread, key_ref[j], NT, preferred_element_type=F32)
        logits += extra_ref[...]
        top = jnp.max(logits, axis=1, keepdims=True)
        expo = jnp.exp(logits - top).astype(BF16)
        both = jnp.dot(
            expo, jnp.concatenate([value_ref[j], ones], axis=1), preferred_element_type=F32
        )
        for b in range(count):
            total = None
            for head in range(heads):
                start = (b * heads + head) * rows
                piece = both[start : start + rows]
                total = piece if total is None else jnp.where(both_head == head, piece, total)
            attended = total[:, :width] / total[:, width:]
            gated.append((gate_ref[first + b, j] * attended).astype(BF16))
    update = []
    for b in range(count):
        value = jnp.dot(
            jnp.concatenate(gated[b::count], axis=0), w_out_ref[...], preferred_element_type=F32
        )
        value = (value + out_shift_ref[...]).astype(BF16).reshape(cols, rows, width)
        update += jnp.split(value, PIECES[first + b], axis=0)
    for ref, value in zip(out_refs, update, strict=True):
        ref[...] = value


def place_kernel(place_ref, *refs):
    part_refs, out_ref, turned_ref = list(refs[:-2]), refs[-2], refs[-1]
    quarter = turned_ref.shape[0] // SPLIT
    for step in range(SPLIT):
        start = jnp.bitwise_xor(place_ref[0] % SPLIT, step) * quarter
        count = quarter // PIECES[step]
        for piece in range(PIECES[step]):
            part = part_refs.pop(0)[...].astype(F32)
            turned_ref[pl.ds(start + piece * count, count)] = part
    out_ref[...] = jnp.swapaxes(turned_ref[...], 0, 1).astype(BF16)


def whole():
    return pl.BlockSpec(memory_space=pltpu.VMEM)


def scalars():
    return pl.BlockSpec(memory_space=pltpu.SMEM)


def on_device(
    row_count,
    col_count,
    pair,
    residue_mask,
    chain_index,
    norm_gain,
    norm_shift,
    w_proj,
    gate_shift,
    w_bias,
    inter_chain,
    w_out,
    out_shift,
):
    rows, cols, channels = pair.shape
    heads = w_bias.shape[1]
    width = w_out.shape[0]
    keys = residue_mask.shape[0]
    quarter = cols // SPLIT
    lanes = heads * rows
    me = lax.axis_index("row")
    place = me[None]

    def swap(value, bit):
        return lax.ppermute(value, "row", [(i, i ^ bit) for i in range(row_count)])

    part = jax.ShapeDtypeStruct((2, quarter, rows, channels), BF16)
    mine, away, bias_copies = pl.pallas_call(
        norm_kernel,
        out_shape=[
            part,
            part,
            jax.ShapeDtypeStruct((col_count, rows, heads * cols), BF16),
        ],
        in_specs=[scalars()] + [whole()] * 4,
        out_specs=[whole()] * 3,
        scratch_shapes=[pltpu.VMEM((cols, rows, channels), BF16)],
        cost_estimate=cost(2 * rows * cols * channels * lanes),
    )(place, pair, norm_gain[None], norm_shift[None], w_bias.T)

    near = jnp.concatenate([mine, swap(away, 2)])
    bias_row = lax.all_to_all(bias_copies, "col", 0, 0, tiled=True)
    gathered = [swap(near, step * SPLIT) for step in range(1, row_count // SPLIT)]

    gate_open = swap(near[3], 1)
    bias_row, gate_open = lax.optimization_barrier((bias_row, gate_open))
    groups = row_count // SPLIT
    bias_chunks = pl.pallas_call(
        copy_kernel,
        out_shape=jax.ShapeDtypeStruct((groups, 2, 2, 2, rows, lanes), BF16),
        in_specs=[whole()],
        out_specs=whole(),
        compiler_params=PARAMS,
        cost_estimate=cost(0),
    )(bias_row.reshape(groups, 2, 2, rows, lanes)).reshape(row_count, 2, rows, lanes)
    bias_here = lax.all_to_all(bias_chunks, "row", 0, 0, tiled=True)

    wq, wk, wv, wg = (w_proj[:, i * width : (i + 1) * width] for i in range(4))
    small = [
        jnp.concatenate([wk, wv, wq, wg], axis=1),
        gate_shift[None],
        residue_mask[None],
        chain_index[None],
        inter_chain[None],
        w_out,
        out_shift[None],
    ]
    everything, chain_query, other, rest, *small = pl.pallas_call(
        gather_kernel,
        out_shape=[
            jax.ShapeDtypeStruct((row_count // SPLIT, 2, quarter, rows, channels), BF16),
            jax.ShapeDtypeStruct((SPLIT, 1, lanes), F32),
            jax.ShapeDtypeStruct((row_count // SPLIT, quarter, rows, channels), BF16),
            jax.ShapeDtypeStruct((row_count // SPLIT, quarter, rows, channels), BF16),
        ]
        + [jax.ShapeDtypeStruct(x.shape, x.dtype) for x in small],
        in_specs=[scalars()] + [whole()] * (SPLIT + len(small)),
        out_specs=[whole()] * (4 + len(small)),
        compiler_params=PARAMS,
        cost_estimate=cost(20 * BUSY),
    )(place, near, *gathered, *small)
    other, rest = swap(other, 1), swap(rest, 1)
    everything, bias_here = lax.optimization_barrier((everything, bias_here))
    bias_there = swap(bias_here, 1)
    *small, w_out, out_shift = small
    projected = jax.ShapeDtypeStruct((quarter, keys, width), BF16)
    key, value, query, gate, side = pl.pallas_call(
        functools.partial(project_kernel, size=width // heads),
        out_shape=[
            projected,
            projected,
            jax.ShapeDtypeStruct((SPLIT, quarter, rows, width), BF16),
            jax.ShapeDtypeStruct((SPLIT, quarter, rows, width), F32),
            jax.ShapeDtypeStruct((SPLIT, lanes, keys), F32),
        ],
        in_specs=[scalars()] + [whole()] * 9,
        out_specs=[whole()] * 5,
        compiler_params=PARAMS,
        cost_estimate=cost(2 * BUSY),
    )(place, everything, other, rest, *small, chain_query)

    def attend(first, count, place, load):
        return pl.pallas_call(
            functools.partial(attend_kernel, heads=heads, first=first, count=count),
            out_shape=[
                jax.ShapeDtypeStruct((quarter // pieces, rows, channels), BF16)
                for pieces in PIECES[first : first + count]
                for _ in range(pieces)
            ],
            in_specs=[scalars()] + [whole()] * 9,
            out_specs=[whole()] * sum(PIECES[first : first + count]),
            scratch_shapes=[pltpu.VMEM((count * lanes, keys), F32)],
            compiler_params=PARAMS,
            cost_estimate=load,
        )(place, query, gate, key, value, bias_here, bias_there, side, w_out, out_shift)

    two, three = attend(2, 2, place, cost(8 * BUSY))
    two, three, later = lax.optimization_barrier((two, three, place))
    two, three = swap(two, 2), swap(three, 3)
    one = attend(1, 1, later, cost(8 * BUSY))
    *one, last = lax.optimization_barrier((*one, place))
    one = [swap(piece, 1) for piece in one]
    (own,) = attend(0, 1, last, cost(0, size=0))
    return pl.pallas_call(
        place_kernel,
        out_shape=jax.ShapeDtypeStruct((rows, cols, channels), BF16),
        in_specs=[scalars()] + [whole()] * sum(PIECES),
        out_specs=whole(),
        scratch_shapes=[pltpu.VMEM((cols, rows, channels), F32)],
        compiler_params=PARAMS,
        cost_estimate=cost(0),
    )(place, own, *one, two, three)


def solution(mesh):
    in_specs = (P("row", "col", None), P(), P(), P(), P(), P(), P(), P(), P(), P(), P())
    out_specs = P("row", "col", None)
    return jax.shard_map(
        functools.partial(on_device, mesh.shape["row"], mesh.shape["col"]),
        mesh=mesh,
        in_specs=in_specs,
        out_specs=out_specs,
        check_vma=False,
    )
```
